32 devices in a mesh: seq: 16 (over z, x, core), head: 2 (over y).
Axes of the slice: x: 2, y: 2, z: 4, core: 2. Of those that a mesh axis runs over, the one named last changes fastest.
Arguments:
- rotated_queries: bfloat16 [8192, 4096], P(('seq', 'head')), may hold values from -6 to 6
- rotated_keys: bfloat16 [8192, 2048], P(('seq', 'head')), may hold values from -6 to 6
- value_matrix: bfloat16 [8192, 2048], P(('seq', 'head')), may hold values from -6 to 6
- output_rows: bfloat16 [8192, 4096], P(('seq', 'head')), may hold values from -6 to 6
- output_gradient: bfloat16 [8192, 4096], P(('seq', 'head')), may hold values from -6 to 6
- softmax_log_total: float32 [32, 8192], P(None, ('seq', 'head')), may hold values from 4 to 7
- doc_ids: int32 [8192], replicated, may hold values from 0 to 8, never falling along the last dimension, each value on 1 to 2048 neighbouring positions
Outputs:
- query_grad: bfloat16 [8192, 4096], P('seq', 'head')
- key_grad: bfloat16 [8192, 2048], P('seq', 'head')
- value_grad: bfloat16 [8192, 2048], P('seq', 'head')
The draws below stay inside these ranges and needn't reach their ends.
Inputs may be any that keep to these rules, and one draw needn't show every extreme that they name: `doc_ids`: ids never fall from one token to the next; no document is longer than 2048 tokens.
All inputs are finite; a program needn't handle non-finite values.
Results may differ from the reference program's by a relative error of at most 0.0055.
Values may be sent and summed in bfloat16 or wider, within the bound.
A program may use at most 128 MiB of HBM per device.

```python
import math
import jax
import jax.numpy as jnp
import numpy as np
from jax import lax

QUERY_HEADS = 32
KEY_VALUE_HEADS = 16
HEAD_SIZE = 128
LOOKBACK_SPAN = 1024
SEQUENCE_TOKENS = 512
SLAB_TOKENS = 8192


def level_of(rng, dims, shards, low, top_value):
    def one(axis_at, blocks):
        heights = jax.random.uniform(jax.random.fold_in(jax.random.fold_in(rng, 6), axis_at), (blocks,), jnp.float32, low / len(shards), top_value / len(shards))
        return jnp.repeat(jnp.exp(heights), dims[axis_at] // blocks).reshape((-1,) + (1,) * (len(dims) - axis_at - 1))

    factor_of = one(*shards[0])
    for cut in shards[1:]:
        factor_of = factor_of * one(*cut)
    return factor_of


def profile(count, total, bound, slope):
    loads = [(1 << 20) // math.isqrt(rank ** slope) + 1 for rank in range(2, count + 1)]
    spare, given = total - bound - (count - 1), [1] * (count - 1)
    while spare > 0:
        free = [i for i in range(count - 1) if given[i] < bound]
        whole, budget = sum([loads[i] for i in free]), spare
        for i in free:
            addition = min(bound - given[i], max(1, budget * loads[i] // whole), spare)
            given[i] = given[i] + addition
            spare = spare - addition
    return np.array([bound] + given)


def ragged_sizes(key, amount, total, limit, skew):
    if amount == 2:
        one = jax.random.randint(key, (), max(1, total - limit), min(limit, total - 1) + 1)
        return jnp.stack([one, total - one])
    lengths = jnp.asarray(profile(amount, total, limit, skew), jnp.int32)
    pairs = (amount - 1) // 2
    source_of, receiver = lengths[1:1 + 2 * pairs:2], lengths[2:2 + 2 * pairs:2]
    margin = jnp.minimum(source_of - 1, limit - receiver)
    passed = jax.random.randint(jax.random.fold_in(key, 1), (pairs,), 0, 1 << 20) % (margin + 1)
    lengths = lengths.at[1:1 + 2 * pairs:2].set(source_of - passed).at[2:2 + 2 * pairs:2].set(receiver + passed)
    return lengths[jax.random.permutation(jax.random.fold_in(key, 2), amount)]


def centred(rng, shape, deviation, limit, split=(), kind=jnp.bfloat16):
    result = jax.random.normal(rng, shape, jnp.float32) * deviation
    if len(split) > 0:
        result = level_of(rng, shape, split, -0.22, 0.18) * result
    return jnp.clip(result, min=-limit, max=limit).astype(kind)


def setup_inputs(seed: int = 0) -> dict:
    splits = jax.random.split(jax.random.key(seed), 8)
    rotated_queries = centred(splits[0], (SLAB_TOKENS, QUERY_HEADS * HEAD_SIZE), 1.0, 6.0, ((0, 32),))
    rotated_keys = centred(splits[1], (SLAB_TOKENS, KEY_VALUE_HEADS * HEAD_SIZE), 1.0, 6.0, ((0, 32),))
    value_matrix = centred(splits[2], (SLAB_TOKENS, KEY_VALUE_HEADS * HEAD_SIZE), 1.0, 6.0, ((0, 32),))
    output_rows = centred(splits[3], (SLAB_TOKENS, QUERY_HEADS * HEAD_SIZE), 1.0, 6.0, ((0, 32),))
    output_gradient = centred(splits[4], (SLAB_TOKENS, QUERY_HEADS * HEAD_SIZE), 1.0, 6.0, ((0, 32),))
    softmax_log_total = jnp.clip(4.0 + 3.0 * jax.random.uniform(splits[5], (QUERY_HEADS, SLAB_TOKENS), jnp.float32) ** level_of(splits[5], (QUERY_HEADS, SLAB_TOKENS), ((1, 32),), -0.2, 0.2), 4.0, 7.0)
    doc_ids = jnp.searchsorted(jnp.cumsum(ragged_sizes(splits[6], SLAB_TOKENS // (2 * SEQUENCE_TOKENS) + 1, SLAB_TOKENS, 4 * SEQUENCE_TOKENS, 2)), jnp.arange(SLAB_TOKENS), side="right").astype(jnp.int32)
    return dict(rotated_queries=rotated_queries, rotated_keys=rotated_keys, value_matrix=value_matrix, output_rows=output_rows, output_gradient=output_gradient, softmax_log_total=softmax_log_total, doc_ids=doc_ids)


score_scale = 168.0 ** -0.5


def reference(rotated_queries, rotated_keys, value_matrix, output_rows, output_gradient, softmax_log_total, doc_ids):
    number_of_tokens = rotated_queries.shape[0]
    window_extent = LOOKBACK_SPAN + SEQUENCE_TOKENS
    query_group_width = QUERY_HEADS // KEY_VALUE_HEADS
    delta_sum = jnp.einsum("thd,thd->ht", output_gradient.astype(jnp.float32).reshape(number_of_tokens, QUERY_HEADS, HEAD_SIZE),
                       output_rows.astype(jnp.float32).reshape(number_of_tokens, QUERY_HEADS, HEAD_SIZE))
    padded_keys = jnp.concatenate([jnp.zeros((LOOKBACK_SPAN, KEY_VALUE_HEADS * HEAD_SIZE), rotated_keys.dtype), rotated_keys], axis=0)
    padded_values = jnp.concatenate([jnp.zeros((LOOKBACK_SPAN, KEY_VALUE_HEADS * HEAD_SIZE), value_matrix.dtype), value_matrix], axis=0)
    doc_pad = jnp.concatenate([jnp.full((LOOKBACK_SPAN,), -1, jnp.int32), doc_ids.astype(jnp.int32)], axis=0)

    def one_block(carried, block_index):
        key_acc, value_acc = carried
        first_row_index = (block_index * SEQUENCE_TOKENS).astype(jnp.int32)
        query_piece = lax.dynamic_slice_in_dim(rotated_queries, first_row_index, SEQUENCE_TOKENS, 0).astype(jnp.float32).reshape(SEQUENCE_TOKENS, KEY_VALUE_HEADS, query_group_width, HEAD_SIZE)
        gradient_piece = lax.dynamic_slice_in_dim(output_gradient, first_row_index, SEQUENCE_TOKENS, 0).astype(jnp.float32).reshape(SEQUENCE_TOKENS, KEY_VALUE_HEADS, query_group_width, HEAD_SIZE)
        logsumexp_piece = lax.dynamic_slice_in_dim(softmax_log_total, first_row_index, SEQUENCE_TOKENS, 1).reshape(KEY_VALUE_HEADS, query_group_width, SEQUENCE_TOKENS)
        delta_piece = lax.dynamic_slice_in_dim(delta_sum, first_row_index, SEQUENCE_TOKENS, 1).reshape(KEY_VALUE_HEADS, query_group_width, SEQUENCE_TOKENS)
        key_piece = lax.dynamic_slice_in_dim(padded_keys, first_row_index, window_extent, 0).astype(jnp.float32).reshape(window_extent, KEY_VALUE_HEADS, HEAD_SIZE)
        value_piece = lax.dynamic_slice_in_dim(padded_values, first_row_index, window_extent, 0).astype(jnp.float32).reshape(window_extent, KEY_VALUE_HEADS, HEAD_SIZE)
        query_doc = lax.dynamic_slice_in_dim(doc_ids.astype(jnp.int32), first_row_index, SEQUENCE_TOKENS, 0)
        key_doc = lax.dynamic_slice_in_dim(doc_pad, first_row_index, window_extent, 0)
        query_pos = jnp.arange(SEQUENCE_TOKENS, dtype=jnp.int32) + LOOKBACK_SPAN
        key_pos = jnp.arange(window_extent, dtype=jnp.int32)
        gap = query_pos[:, None] - key_pos[None, :]
        allowed = (gap >= 0) & (gap < LOOKBACK_SPAN) & (query_doc[:, None] == key_doc[None, :])
        scores = jnp.einsum("rgad,cgd->garc", query_piece, key_piece) * score_scale
        prob_full = jnp.where(allowed[None, None], jnp.exp(scores - logsumexp_piece[..., None]), 0.0)
        probability_narrow = lax.optimization_barrier(prob_full.astype(jnp.bfloat16)).astype(jnp.float32)
        prob_grad = jnp.einsum("rgad,cgd->garc", gradient_piece, value_piece)
        score_gradient = (score_scale * prob_full * (prob_grad - delta_piece[..., None])).astype(jnp.bfloat16)
        score_gradient = lax.optimization_barrier(score_gradient).astype(jnp.float32)
        query_part = jnp.einsum("garc,cgd->rgad", score_gradient, key_piece).reshape(SEQUENCE_TOKENS, QUERY_HEADS * HEAD_SIZE)
        key_portion = jnp.einsum("plmw,mplo->wpo", score_gradient, query_piece).reshape(window_extent, KEY_VALUE_HEADS * HEAD_SIZE)
        value_portion = jnp.einsum("plmw,mplo->wpo", probability_narrow, gradient_piece).reshape(window_extent, KEY_VALUE_HEADS * HEAD_SIZE)
        key_acc = lax.dynamic_update_slice_in_dim(key_acc, lax.dynamic_slice_in_dim(key_acc, first_row_index, window_extent, 0) + key_portion, first_row_index, 0)
        value_acc = lax.dynamic_update_slice_in_dim(value_acc, lax.dynamic_slice_in_dim(value_acc, first_row_index, window_extent, 0) + value_portion, first_row_index, 0)
        return (key_acc, value_acc), query_part.astype(jnp.bfloat16)

    zero_accumulator = jnp.zeros((number_of_tokens + LOOKBACK_SPAN, KEY_VALUE_HEADS * HEAD_SIZE), jnp.float32)
    block_total = number_of_tokens // SEQUENCE_TOKENS
    (key_acc, value_acc), query_blocks = lax.scan(one_block, (zero_accumulator, zero_accumulator), jnp.arange(block_total, dtype=jnp.int32))
    query_grad = query_blocks.reshape(number_of_tokens, QUERY_HEADS * HEAD_SIZE)
    return query_grad, key_acc[LOOKBACK_SPAN:].astype(jnp.bfloat16), value_acc[LOOKBACK_SPAN:].astype(jnp.bfloat16)
```

```python
import functools
import math

import jax
import jax.numpy as jnp
from jax import lax
from jax.experimental import pallas as pl
from jax.experimental.pallas import tpu as pltpu
from jax.sharding import PartitionSpec as P

HEAD_SIZE = 128
LOOKBACK_SPAN = 1024
TILE = 256
SCORE_SCALE = 168.0 ** (-0.5)
LOG2E = math.log2(math.e)
MASKED = -1e30
MESH = pl.DeviceIdType.MESH
Y_LEAD = 4
HALO_LEAD = 2


def dot(a, b, contract):
    return lax.dot_general(a, b, ((contract[:1], contract[1:]), ((), ())), preferred_element_type=jnp.float32)


def kernel(
    shards, parts, heads,
    q_hbm, k_hbm, v_hbm, do_hbm, stats_hbm, docs_ref,
    dq_ref, dk_ref, dv_ref,
    kv, qd, stats, bias, own, acc, dqt, part, ret_a, ret_b, ret_c,
    y_send, y_recv, loc, st_send, st_recv, st_loc,
    near_send, near_recv, fardir_send, fwd_send, far_recv,
    p0_send, p1_send, a_recv, b_recv, c_recv,
):
    s = lax.axis_index("seq")
    y = lax.axis_index("head")
    even = lax.rem(s, 2) == 0
    rows = k_hbm.shape[0]
    block = rows * parts
    near_rows = pl.ds(block, block)
    far_rows = pl.ds(0, block)
    own_rows = pl.ds(2 * block, block)

    def at(seq, head):
        return {"seq": seq, "head": head}

    barrier = pltpu.get_barrier_semaphore()
    for step in range(1, parts):
        pl.semaphore_signal(barrier, inc=1, device_id=at(s, lax.rem(y + step, parts)), device_id_type=MESH)
    has_prev, has_next = s >= 1, s < shards - 1
    even_prev = even & (s >= 2)
    even_next = even & (s + 2 < shards)
    for cond, other in ((has_prev, s - 1), (has_next, s + 1), (even_prev, s - 2), (even_next, s + 2)):

        @pl.when(cond)
        def _():
            pl.semaphore_signal(barrier, inc=1, device_id=at(other, y), device_id_type=MESH)

    peers = parts - 1
    for cond in (has_prev, has_next, even_prev, even_next):
        peers = peers + jnp.where(cond, 1, 0)
    pl.semaphore_wait(barrier, peers)

    half = (y * rows) // TILE
    inner = pl.multiple_of(lax.rem(y * rows, TILE), rows)
    token_row = pl.multiple_of(2 * block + y * rows, rows)

    def pieces(g, target):
        head = target * heads + g
        col = pl.ds(pl.multiple_of(head * HEAD_SIZE, HEAD_SIZE), HEAD_SIZE)
        found = [
            (k_hbm.at[:, col], kv.at[g, 0, pl.ds(token_row, rows), :]),
            (v_hbm.at[:, col], kv.at[g, 1, pl.ds(token_row, rows), :]),
        ]
        for source, slot in ((q_hbm, 0), (do_hbm, 1)):
            for j in range(2):
                qcol = pl.ds(pl.multiple_of((head * 2 + j) * HEAD_SIZE, HEAD_SIZE), HEAD_SIZE)
                found.append((source.at[:, qcol], qd.at[g, slot, half, j, pl.ds(inner, rows), :]))
        return found

    def y_copies(g, which):
        found = []
        for step in range(1, parts):
            target = lax.rem(y + step, parts)
            for n, (src, dst) in enumerate(pieces(g, target)):
                if n in which:
                    found.append(
                        pltpu.make_async_remote_copy(
                            src_ref=src, dst_ref=dst,
                            send_sem=y_send.at[g, step, n], recv_sem=y_recv.at[g, step, n],
                            device_id=at(s, target), device_id_type=MESH,
                        )
                    )
        return found

    def local_copies(g, which):
        return [
            pltpu.make_async_copy(src, dst, loc.at[g, n])
            for n, (src, dst) in enumerate(pieces(g, y))
            if n in which
        ]

    KV_PIECES, Q_PIECES = (0, 1), (2, 3, 4, 5)

    def y_start(g, which):
        for copy in y_copies(g, which):
            copy.start()
        for copy in local_copies(g, which):
            copy.start()

    def y_arrive(g, which):
        for step in range(1, parts):
            source = lax.rem(y + parts - step, parts)
            their_half = (source * rows) // TILE
            their_inner = pl.multiple_of(lax.rem(source * rows, TILE), rows)
            their_row = pl.multiple_of(2 * block + source * rows, rows)
            for n, (src, _) in enumerate(pieces(g, y)):
                if n not in which:
                    continue
                if n < 2:
                    dst = kv.at[g, n, pl.ds(their_row, rows), :]
                else:
                    dst = qd.at[g, (n - 2) // 2, their_half, (n - 2) % 2, pl.ds(their_inner, rows), :]
                pltpu.make_async_remote_copy(
                    src_ref=src, dst_ref=dst,
                    send_sem=y_send.at[g, step, n], recv_sem=y_recv.at[g, step, n],
                    device_id=at(s, source), device_id_type=MESH,
                ).wait_recv()
        for copy in local_copies(g, which):
            copy.wait()

    def stat_copy(step, mine):
        other = lax.rem(y + step, parts)
        source = y if mine else lax.rem(y + parts - step, parts)
        return pltpu.make_async_remote_copy(
            src_ref=stats_hbm.at[other], dst_ref=stats.at[source],
            send_sem=st_send.at[step], recv_sem=st_recv.at[step],
            device_id=at(s, other), device_id_type=MESH,
        )

    def remote(src, dst, send, recv, target):
        return pltpu.make_async_remote_copy(
            src_ref=src, dst_ref=dst, send_sem=send, recv_sem=recv,
            device_id=at(target, y), device_id_type=MESH,
        )

    def near(g):
        return remote(kv.at[g, :, own_rows, :], kv.at[g, :, near_rows, :], near_send.at[g], near_recv.at[g], s + 1)

    def far_direct(g):
        return remote(kv.at[g, :, own_rows, :], kv.at[g, :, far_rows, :], fardir_send.at[g], far_recv.at[g], s + 2)

    def far_forward(g):
        return remote(kv.at[g, :, near_rows, :], kv.at[g, :, far_rows, :], fwd_send.at[g], far_recv.at[g], s + 1)

    def back_far_even(g):
        return remote(part.at[g, 0], ret_b.at[g], p0_send.at[g], b_recv.at[g], s - 2)

    def back_far_odd(g):
        return remote(part.at[g, 0], ret_c.at[g], p0_send.at[g], c_recv.at[g], s - 1)

    def back_near(g):
        return remote(part.at[g, 1], ret_a.at[g], p1_send.at[g], a_recv.at[g], s - 1)

    def halo_send(g):
        y_arrive(g, KV_PIECES)

        @pl.when(has_next)
        def _():
            near(g).start()

        @pl.when(even_next)
        def _():
            far_direct(g).start()

    lead = min(Y_LEAD, heads)
    halo_lead = min(HALO_LEAD, heads)
    y_start(0, KV_PIECES)
    for step in range(1, parts):
        stat_copy(step, True).start()
    stat_local = pltpu.make_async_copy(stats_hbm.at[y], stats.at[y], st_loc.at[0])
    stat_local.start()
    for g in range(1, lead):
        y_start(g, KV_PIECES)
        y_start(g - 1, Q_PIECES)
    y_start(lead - 1, Q_PIECES)

    for limit, row in ((2, 0), (1, block)):

        @pl.when(s < limit)
        def _():
            @pl.loop(0, heads)
            def _(g):
                kv[g, :, pl.ds(row, block), :] = jnp.zeros((2, block, HEAD_SIZE), kv.dtype)

    key_tiles = 3 * block // TILE
    reach = LOOKBACK_SPAN // TILE

    def pair_index(t, u):
        return u * (reach + 1) + (t - u)

    for t in range(key_tiles):
        key_doc = jnp.broadcast_to(docs_ref[:, t * TILE:(t + 1) * TILE], (TILE, TILE)).T
        for u in range(2):
            if not 0 <= t - u <= reach:
                continue
            first = 2 * block + u * TILE
            query_doc = docs_ref[:, first:first + TILE]
            gap = (
                (first - t * TILE)
                + lax.broadcasted_iota(jnp.int32, (TILE, TILE), 1)
                - lax.broadcasted_iota(jnp.int32, (TILE, TILE), 0)
            )
            allowed = (key_doc == query_doc) & (gap >= 0) & (gap < LOOKBACK_SPAN)
            bias[pair_index(t, u)] = jnp.where(allowed, 0.0, MASKED)

    for g in range(halo_lead):
        halo_send(g)
    for step in range(1, parts):
        stat_copy(step, False).wait_recv()
    stat_local.wait()

    sources = parts // 2

    def stat_row(g, u, kind):
        found = [
            stats[u * sources + i, g, kind * 2 + j:kind * 2 + j + 1, :]
            for j in range(2)
            for i in range(sources)
        ]
        return jnp.concatenate(found, axis=1) if len(found) > 1 else found[0]

    def tile(g, t, u):
        keys = kv[g, 0, t * TILE:(t + 1) * TILE, :]
        values = kv[g, 1, t * TILE:(t + 1) * TILE, :]
        queries = qd[g, 0, u].reshape(2 * TILE, HEAD_SIZE)
        grads = qd[g, 1, u].reshape(2 * TILE, HEAD_SIZE)
        mask = bias[pair_index(t, u)]
        scores = dot(keys, queries, (1, 1)) * (SCORE_SCALE * LOG2E) - stat_row(g, u, 0)
        prob = jnp.exp2(scores + jnp.concatenate([mask, mask], axis=1))
        prob_grad = dot(values, grads, (1, 1))
        score_grad = (SCORE_SCALE * prob * (prob_grad - stat_row(g, u, 1))).astype(jnp.bfloat16)
        dv = dot(prob.astype(jnp.bfloat16), grads, (1, 0))
        dk = dot(score_grad, queries, (1, 0))
        dq = dot(keys, score_grad, (0, 0))
        if t == u:
            dqt[u] = dq
        else:
            dqt[u] += dq
        first = u == 0 or t == reach + 1
        if t < 2 * block // TILE:
            target, row = acc, t * TILE
        else:
            target, row = own.at[g], t * TILE - 2 * block
        if first:
            target[0, row:row + TILE, :] = dk
            target[1, row:row + TILE, :] = dv
        else:
            target[0, row:row + TILE, :] += dk
            target[1, row:row + TILE, :] += dv

    def combine(g):
        back_far_odd(g).wait_recv()
        part[g, 1] = (part[g, 1].astype(jnp.float32) + ret_c[g].astype(jnp.float32)).astype(jnp.bfloat16)
        back_near(g).start()

    @pl.loop(0, heads)
    def _(g):
        @pl.when(g + lead < heads)
        def _():
            y_start(g + lead, KV_PIECES)
            y_start(g + lead, Q_PIECES)

        @pl.when(g + halo_lead < heads)
        def _():
            halo_send(g + halo_lead)

        @pl.when(has_prev)
        def _():
            near(g).wait_recv()

        @pl.when(even_prev)
        def _():
            far_forward(g).start()

        y_arrive(g, Q_PIECES)

        @pl.when(s >= 2)
        def _():
            far_direct(g).wait_recv()

        own_tile = 2 * block // TILE
        for u in range(2):
            for t in range(u, own_tile):
                tile(g, t, u)
        part[g, 0] = acc[:, 0:block, :].astype(jnp.bfloat16)
        part[g, 1] = acc[:, block:2 * block, :].astype(jnp.bfloat16)

        @pl.when(even_prev)
        def _():
            back_far_even(g).start()

        @pl.when(jnp.logical_not(even))
        def _():
            back_near(g).start()

        @pl.when(jnp.logical_not(even) & (s >= 2))
        def _():
            back_far_odd(g).start()

        for t, u in ((own_tile, 0), (own_tile, 1), (own_tile + 1, 1)):
            tile(g, t, u)
        for u in range(2):
            for j in range(2):
                head_cols = pl.ds(pl.multiple_of((g * 2 + j) * HEAD_SIZE, HEAD_SIZE), HEAD_SIZE)
                dq_ref[u * TILE:(u + 1) * TILE, head_cols] = (
                    dqt[u, :, j * TILE:(j + 1) * TILE].T.astype(jnp.bfloat16)
                )

        @pl.when(even_prev & (g >= 1))
        def _():
            combine(g - 1)

    @pl.when(even_prev)
    def _():
        combine(heads - 1)

    @pl.loop(0, heads)
    def _(g):
        @pl.when(has_next)
        def _():
            back_near(g).wait_recv()
            own[g] += ret_a[g].astype(jnp.float32)

        @pl.when(even_next)
        def _():
            back_far_even(g).wait_recv()
            own[g] += ret_b[g].astype(jnp.float32)

        cols = pl.ds(pl.multiple_of(g * HEAD_SIZE, HEAD_SIZE), HEAD_SIZE)
        dk_ref[:, cols] = own[g, 0].astype(jnp.bfloat16)
        dv_ref[:, cols] = own[g, 1].astype(jnp.bfloat16)

    @pl.loop(0, heads)
    def _(g):
        for copy in y_copies(g, KV_PIECES + Q_PIECES):
            copy.wait_send()

        @pl.when(has_next)
        def _():
            near(g).wait_send()

        @pl.when(even_next)
        def _():
            far_direct(g).wait_send()

        @pl.when(even_prev)
        def _():
            far_forward(g).wait_send()

        @pl.when(s >= 2)
        def _():
            back_far_even(g).wait_send()

        @pl.when(has_prev)
        def _():
            back_near(g).wait_send()

    for step in range(1, parts):
        stat_copy(step, True).wait_send()


def on_device(
    shards, parts,
    rotated_queries, rotated_keys, value_matrix, output_rows, output_gradient, softmax_log_total, doc_ids,
):
    rows = rotated_queries.shape[0]
    query_heads = softmax_log_total.shape[0]
    key_heads = rotated_keys.shape[1] // HEAD_SIZE
    heads = key_heads // parts
    block = rows * parts
    delta = jnp.sum(
        (output_gradient.astype(jnp.float32) * output_rows.astype(jnp.float32)).reshape(rows, query_heads, HEAD_SIZE),
        axis=2,
    ).T
    stats = jnp.concatenate(
        [
            (softmax_log_total * LOG2E).reshape(parts, heads, 2, rows),
            delta.reshape(parts, heads, 2, rows),
        ],
        axis=2,
    )
    padded = jnp.concatenate([jnp.full((LOOKBACK_SPAN,), -1.0, jnp.float32), doc_ids.astype(jnp.float32)])
    docs = lax.dynamic_slice_in_dim(padded, lax.axis_index("seq") * block, 3 * block, 0)[None, :]

    any_spec = pl.BlockSpec(memory_space=pl.ANY)
    vmem = pl.BlockSpec(memory_space=pltpu.VMEM)
    dma = pltpu.SemaphoreType.DMA
    bf16, f32 = jnp.bfloat16, jnp.float32
    back = pltpu.VMEM((heads, 2, block, HEAD_SIZE), bf16)
    pairs = 2 * (LOOKBACK_SPAN // TILE + 1)
    pair_ops = heads * pairs * TILE * 2 * TILE
    return pl.pallas_call(
        functools.partial(kernel, shards, parts, heads),
        out_shape=(
            jax.ShapeDtypeStruct((block, heads * 2 * HEAD_SIZE), bf16),
            jax.ShapeDtypeStruct((block, heads * HEAD_SIZE), bf16),
            jax.ShapeDtypeStruct((block, heads * HEAD_SIZE), bf16),
        ),
        in_specs=[any_spec] * 5 + [vmem],
        out_specs=(vmem, vmem, vmem),
        scratch_shapes=[
            pltpu.VMEM((heads, 2, 3 * block, HEAD_SIZE), bf16),
            pltpu.VMEM((heads, 2, 2, 2, TILE, HEAD_SIZE), bf16),
            pltpu.VMEM((parts, heads, 4, rows), f32),
            pltpu.VMEM((pairs, TILE, TILE), f32),
            pltpu.VMEM((heads, 2, block, HEAD_SIZE), f32),
            pltpu.VMEM((2, 2 * block, HEAD_SIZE), f32),
            pltpu.VMEM((2, HEAD_SIZE, 2 * TILE), f32),
            pltpu.VMEM((heads, 2, 2, block, HEAD_SIZE), bf16),
            back, back, back,
            dma((heads, parts, 6)), dma((heads, parts, 6)), dma((heads, 6)),
            dma((parts,)), dma((parts,)), dma((1,)),
        ] + [dma((heads,))] * 10,
        compiler_params=pltpu.CompilerParams(
            collective_id=0, has_side_effects=True, vmem_limit_bytes=52 * 2 ** 20
        ),
        cost_estimate=pl.CostEstimate(
            flops=pair_ops * HEAD_SIZE * 10, bytes_accessed=16 * 2 ** 20, transcendentals=pair_ops
        ),
    )(rotated_queries, rotated_keys, value_matrix, output_gradient, stats, docs)


def solution(mesh):
    return jax.shard_map(
        functools.partial(on_device, mesh.shape["seq"], mesh.shape["head"]),
        mesh=mesh,
        in_specs=(
            P(("seq", "head"), None),
            P(("seq", "head"), None),
            P(("seq", "head"), None),
            P(("seq", "head"), None),
            P(("seq", "head"), None),
            P(None, ("seq", "head")),
            P(),
        ),
        out_specs=(P("seq", "head"), P("seq", "head"), P("seq", "head")),
        check_vma=False,
    )
```

```python
import functools
import math

import jax
import jax.numpy as jnp
from jax import lax
from jax.experimental import pallas as pl
from jax.experimental.pallas import tpu as pltpu
from jax.sharding import PartitionSpec as P

HEAD_SIZE = 128
LOOKBACK_SPAN = 1024
TILE = 256
SCORE_SCALE = 168.0 ** (-0.5)
LOG2E = math.log2(math.e)
MASKED = -1e30
MESH = pl.DeviceIdType.MESH
KV_LEAD = 5
Q_LEAD = 2
HALO_LEAD = 3


def dot(a, b, contract):
    return lax.dot_general(a, b, ((contract[:1], contract[1:]), ((), ())), preferred_element_type=jnp.float32)


def kernel(
    shards, parts, heads,
    q_hbm, k_hbm, v_hbm, do_hbm, o_hbm, lse_ref, docs_ref,
    dq_ref, dk_ref, dv_ref,
    kv, qd, stats, bias, own, acc, dqt, part, ret_a, ret_b, ret_c, o_buf, do_buf, st_src,
    y_send, y_recv, loc, st_send, st_recv, st_loc,
    near_send, near_recv, fardir_send, fwd_send, far_recv,
    p0_send, p1_send, a_recv, b_recv, c_recv,
):
    s = lax.axis_index("seq")
    y = lax.axis_index("head")
    even = lax.rem(s, 2) == 0
    rows = k_hbm.shape[0]
    block = rows * parts
    near_rows = pl.ds(block, block)
    far_rows = pl.ds(0, block)
    own_rows = pl.ds(2 * block, block)

    def at(seq, head):
        return {"seq": seq, "head": head}

    barrier = pltpu.get_barrier_semaphore()
    for step in range(1, parts):
        pl.semaphore_signal(barrier, inc=1, device_id=at(s, lax.rem(y + step, parts)), device_id_type=MESH)
    has_prev, has_next = s >= 1, s < shards - 1
    even_prev = even & (s >= 2)
    even_next = even & (s + 2 < shards)
    for cond, other in ((has_prev, s - 1), (has_next, s + 1), (even_prev, s - 2), (even_next, s + 2)):

        @pl.when(cond)
        def _():
            pl.semaphore_signal(barrier, inc=1, device_id=at(other, y), device_id_type=MESH)

    peers = parts - 1
    for cond in (has_prev, has_next, even_prev, even_next):
        peers = peers + jnp.where(cond, 1, 0)
    pl.semaphore_wait(barrier, peers)

    half = (y * rows) // TILE
    inner = pl.multiple_of(lax.rem(y * rows, TILE), rows)
    token_row = pl.multiple_of(2 * block + y * rows, rows)

    def pieces(g, target):
        head = target * heads + g
        col = pl.ds(pl.multiple_of(head * HEAD_SIZE, HEAD_SIZE), HEAD_SIZE)
        found = [
            (k_hbm.at[:, col], kv.at[g, 0, pl.ds(token_row, rows), :]),
            (v_hbm.at[:, col], kv.at[g, 1, pl.ds(token_row, rows), :]),
        ]
        for source, slot in ((q_hbm, 0), (do_hbm, 1)):
            for j in range(2):
                qcol = pl.ds(pl.multiple_of((head * 2 + j) * HEAD_SIZE, HEAD_SIZE), HEAD_SIZE)
                found.append((source.at[:, qcol], qd.at[g, slot, half, j, pl.ds(inner, rows), :]))
        return found

    def y_copies(g, which):
        found = []
        for step in range(1, parts):
            target = lax.rem(y + step, parts)
            for n, (src, dst) in enumerate(pieces(g, target)):
                if n in which:
                    found.append(
                        pltpu.make_async_remote_copy(
                            src_ref=src, dst_ref=dst,
                            send_sem=y_send.at[g, step, n], recv_sem=y_recv.at[g, step, n],
                            device_id=at(s, target), device_id_type=MESH,
                        )
                    )
        return found

    def local_copies(g, which):
        return [
            pltpu.make_async_copy(src, dst, loc.at[g, n])
            for n, (src, dst) in enumerate(pieces(g, y))
            if n in which
        ]

    KV_PIECES, Q_PIECES = (0, 1), (2, 3, 4, 5)

    def y_start(g, which):
        for copy in y_copies(g, which):
            copy.start()
        for copy in local_copies(g, which):
            copy.start()

    def y_arrive(g, which):
        for step in range(1, parts):
            source = lax.rem(y + parts - step, parts)
            their_half = (source * rows) // TILE
            their_inner = pl.multiple_of(lax.rem(source * rows, TILE), rows)
            their_row = pl.multiple_of(2 * block + source * rows, rows)
            for n, (src, _) in enumerate(pieces(g, y)):
                if n not in which:
                    continue
                if n < 2:
                    dst = kv.at[g, n, pl.ds(their_row, rows), :]
                else:
                    dst = qd.at[g, (n - 2) // 2, their_half, (n - 2) % 2, pl.ds(their_inner, rows), :]
                pltpu.make_async_remote_copy(
                    src_ref=src, dst_ref=dst,
                    send_sem=y_send.at[g, step, n], recv_sem=y_recv.at[g, step, n],
                    device_id=at(s, source), device_id_type=MESH,
                ).wait_recv()
        for copy in local_copies(g, which):
            copy.wait()

    def stat_copy(step, mine):
        other = lax.rem(y + step, parts)
        source = y if mine else lax.rem(y + parts - step, parts)
        return pltpu.make_async_remote_copy(
            src_ref=st_src.at[other], dst_ref=stats.at[source],
            send_sem=st_send.at[step], recv_sem=st_recv.at[step],
            device_id=at(s, other), device_id_type=MESH,
        )

    def remote(src, dst, send, recv, target):
        return pltpu.make_async_remote_copy(
            src_ref=src, dst_ref=dst, send_sem=send, recv_sem=recv,
            device_id=at(target, y), device_id_type=MESH,
        )

    def near(g):
        return remote(kv.at[g, :, own_rows, :], kv.at[g, :, near_rows, :], near_send.at[g], near_recv.at[g], s + 1)

    def far_direct(g):
        return remote(kv.at[g, :, own_rows, :], kv.at[g, :, far_rows, :], fardir_send.at[g], far_recv.at[g], s + 2)

    def far_forward(g):
        return remote(kv.at[g, :, near_rows, :], kv.at[g, :, far_rows, :], fwd_send.at[g], far_recv.at[g], s + 1)

    def back_far_even(g):
        return remote(part.at[g, 0], ret_b.at[g], p0_send.at[g], b_recv.at[g], s - 2)

    def back_far_odd(g):
        return remote(part.at[g, 0], ret_c.at[g], p0_send.at[g], c_recv.at[g], s - 1)

    def back_near(g):
        return remote(part.at[g, 1], ret_a.at[g], p1_send.at[g], a_recv.at[g], s - 1)

    def halo_send(g):
        y_arrive(g, KV_PIECES)

        @pl.when(has_next)
        def _():
            near(g).start()

        @pl.when(even_next)
        def _():
            far_direct(g).start()

    kv_lead, q_lead, halo_lead = (min(n, heads) for n in (KV_LEAD, Q_LEAD, HALO_LEAD))
    y_start(0, KV_PIECES)
    o_copy = pltpu.make_async_copy(o_hbm, o_buf, st_loc.at[0])
    do_copy = pltpu.make_async_copy(do_hbm, do_buf, st_loc.at[1])
    o_copy.start()
    do_copy.start()
    for g in range(1, halo_lead):
        y_start(g, KV_PIECES)

    def fill_stats(p, target):
        @pl.loop(0, heads)
        def _(g):
            target[g, 0:2, :] = lse_ref[p, g] * LOG2E
            for j in range(2):
                cols = pl.ds(pl.multiple_of(((p * heads + g) * 2 + j) * HEAD_SIZE, HEAD_SIZE), HEAD_SIZE)
                product = o_buf[:, cols].astype(jnp.float32) * do_buf[:, cols].astype(jnp.float32)
                target[g, 2 + j:3 + j, :] = jnp.sum(product.T, axis=0, keepdims=True)

    o_copy.wait()
    do_copy.wait()
    for step in range(1, parts):
        other = lax.rem(y + step, parts)
        fill_stats(other, st_src.at[other])
        stat_copy(step, True).start()
    for g in range(halo_lead):
        halo_send(g)
        if g < q_lead:
            y_start(g, Q_PIECES)
        if halo_lead + g < kv_lead:
            y_start(halo_lead + g, KV_PIECES)
    for g in range(halo_lead, q_lead):
        y_start(g, Q_PIECES)
    fill_stats(y, stats.at[y])

    for limit, row in ((2, 0), (1, block)):

        @pl.when(s < limit)
        def _():
            @pl.loop(0, heads)
            def _(g):
                kv[g, :, pl.ds(row, block), :] = jnp.zeros((2, block, HEAD_SIZE), kv.dtype)

    key_tiles = 3 * block // TILE
    reach = LOOKBACK_SPAN // TILE

    def pair_index(t, u):
        return u * (reach + 1) + (t - u)

    for t in range(key_tiles):
        key_doc = jnp.broadcast_to(docs_ref[:, t * TILE:(t + 1) * TILE], (TILE, TILE)).T
        for u in range(2):
            if not 0 <= t - u <= reach:
                continue
            first = 2 * block + u * TILE
            query_doc = docs_ref[:, first:first + TILE]
            gap = (
                (first - t * TILE)
                + lax.broadcasted_iota(jnp.int32, (TILE, TILE), 1)
                - lax.broadcasted_iota(jnp.int32, (TILE, TILE), 0)
            )
            allowed = (key_doc == query_doc) & (gap >= 0) & (gap < LOOKBACK_SPAN)
            bias[pair_index(t, u)] = jnp.where(allowed, 0.0, MASKED)

    for step in range(1, parts):
        stat_copy(step, False).wait_recv()

    sources = parts // 2

    def stat_row(g, u, kind):
        found = [
            stats[u * sources + i, g, kind * 2 + j:kind * 2 + j + 1, :]
            for j in range(2)
            for i in range(sources)
        ]
        return jnp.concatenate(found, axis=1) if len(found) > 1 else found[0]

    def tile(g, t, u):
        keys = kv[g, 0, t * TILE:(t + 1) * TILE, :]
        values = kv[g, 1, t * TILE:(t + 1) * TILE, :]
        queries = qd[g, 0, u].reshape(2 * TILE, HEAD_SIZE)
        grads = qd[g, 1, u].reshape(2 * TILE, HEAD_SIZE)
        mask = bias[pair_index(t, u)]
        scores = dot(keys, queries, (1, 1)) * (SCORE_SCALE * LOG2E) - stat_row(g, u, 0)
        prob = jnp.exp2(scores + jnp.concatenate([mask, mask], axis=1))
        prob_grad = dot(values, grads, (1, 1))
        score_grad = (SCORE_SCALE * prob * (prob_grad - stat_row(g, u, 1))).astype(jnp.bfloat16)
        dv = dot(prob.astype(jnp.bfloat16), grads, (1, 0))
        dk = dot(score_grad, queries, (1, 0))
        dq = dot(keys, score_grad, (0, 0))
        if t == u:
            dqt[u] = dq
        else:
            dqt[u] += dq
        first = u == 0 or t == reach + 1
        if t < 2 * block // TILE:
            target, row = acc, t * TILE
        else:
            target, row = own.at[g], t * TILE - 2 * block
        if first:
            target[0, row:row + TILE, :] = dk
            target[1, row:row + TILE, :] = dv
        else:
            target[0, row:row + TILE, :] += dk
            target[1, row:row + TILE, :] += dv

    def combine(g):
        back_far_odd(g).wait_recv()
        part[g, 1] = (part[g, 1].astype(jnp.float32) + ret_c[g].astype(jnp.float32)).astype(jnp.bfloat16)
        back_near(g).start()

    @pl.loop(0, heads)
    def _(g):
        @pl.when(g + kv_lead < heads)
        def _():
            y_start(g + kv_lead, KV_PIECES)

        @pl.when(g + q_lead < heads)
        def _():
            y_start(g + q_lead, Q_PIECES)

        @pl.when(g + halo_lead < heads)
        def _():
            halo_send(g + halo_lead)

        @pl.when(has_prev)
        def _():
            near(g).wait_recv()

        @pl.when(even_prev)
        def _():
            far_forward(g).start()

        y_arrive(g, Q_PIECES)

        @pl.when(s >= 2)
        def _():
            far_direct(g).wait_recv()

        own_tile = 2 * block // TILE
        for u in range(2):
            for t in range(u, own_tile):
                tile(g, t, u)
        part[g, 0] = acc[:, 0:block, :].astype(jnp.bfloat16)
        part[g, 1] = acc[:, block:2 * block, :].astype(jnp.bfloat16)

        @pl.when(even_prev)
        def _():
            back_far_even(g).start()

        @pl.when(jnp.logical_not(even))
        def _():
            back_near(g).start()

        @pl.when(jnp.logical_not(even) & (s >= 2))
        def _():
            back_far_odd(g).start()

        @pl.when(even_prev & (g >= 1))
        def _():
            combine(g - 1)

        for t, u in ((own_tile, 0), (own_tile, 1), (own_tile + 1, 1)):
            tile(g, t, u)
        for u in range(2):
            for j in range(2):
                head_cols = pl.ds(pl.multiple_of((g * 2 + j) * HEAD_SIZE, HEAD_SIZE), HEAD_SIZE)
                dq_ref[u * TILE:(u + 1) * TILE, head_cols] = (
                    dqt[u, :, j * TILE:(j + 1) * TILE].T.astype(jnp.bfloat16)
                )

    @pl.when(even_prev)
    def _():
        combine(heads - 1)

    @pl.loop(0, heads)
    def _(g):
        @pl.when(has_next)
        def _():
            back_near(g).wait_recv()
            own[g] += ret_a[g].astype(jnp.float32)

        @pl.when(even_next)
        def _():
            back_far_even(g).wait_recv()
            own[g] += ret_b[g].astype(jnp.float32)

        cols = pl.ds(pl.multiple_of(g * HEAD_SIZE, HEAD_SIZE), HEAD_SIZE)
        dk_ref[:, cols] = own[g, 0].astype(jnp.bfloat16)
        dv_ref[:, cols] = own[g, 1].astype(jnp.bfloat16)

    @pl.loop(0, heads)
    def _(g):
        for copy in y_copies(g, KV_PIECES + Q_PIECES):
            copy.wait_send()

        @pl.when(has_next)
        def _():
            near(g).wait_send()

        @pl.when(even_next)
        def _():
            far_direct(g).wait_send()

        @pl.when(even_prev)
        def _():
            far_forward(g).wait_send()

        @pl.when(s >= 2)
        def _():
            back_far_even(g).wait_send()

        @pl.when(has_prev)
        def _():
            back_near(g).wait_send()

    for step in range(1, parts):
        stat_copy(step, True).wait_send()


def on_device(
    shards, parts,
    rotated_queries, rotated_keys, value_matrix, output_rows, output_gradient, softmax_log_total, doc_ids,
):
    rows = rotated_queries.shape[0]
    key_heads = rotated_keys.shape[1] // HEAD_SIZE
    heads = key_heads // parts
    block = rows * parts
    lse = softmax_log_total.reshape(parts, heads, 2, rows)
    padded = jnp.concatenate([jnp.full((LOOKBACK_SPAN,), -1.0, jnp.float32), doc_ids.astype(jnp.float32)])
    docs = lax.dynamic_slice_in_dim(padded, lax.axis_index("seq") * block, 3 * block, 0)[None, :]

    any_spec = pl.BlockSpec(memory_space=pl.ANY)
    vmem = pl.BlockSpec(memory_space=pltpu.VMEM)
    dma = pltpu.SemaphoreType.DMA
    bf16, f32 = jnp.bfloat16, jnp.float32
    back = pltpu.VMEM((heads, 2, block, HEAD_SIZE), bf16)
    pairs = 2 * (LOOKBACK_SPAN // TILE + 1)
    pair_ops = heads * pairs * TILE * 2 * TILE
    return pl.pallas_call(
        functools.partial(kernel, shards, parts, heads),
        out_shape=(
            jax.ShapeDtypeStruct((block, heads * 2 * HEAD_SIZE), bf16),
            jax.ShapeDtypeStruct((block, heads * HEAD_SIZE), bf16),
            jax.ShapeDtypeStruct((block, heads * HEAD_SIZE), bf16),
        ),
        in_specs=[any_spec] * 5 + [vmem, vmem],
        out_specs=(vmem, vmem, vmem),
        scratch_shapes=[
            pltpu.VMEM((heads, 2, 3 * block, HEAD_SIZE), bf16),
            pltpu.VMEM((heads, 2, 2, 2, TILE, HEAD_SIZE), bf16),
            pltpu.VMEM((parts, heads, 4, rows), f32),
            pltpu.VMEM((pairs, TILE, TILE), f32),
            pltpu.VMEM((heads, 2, block, HEAD_SIZE), f32),
            pltpu.VMEM((2, 2 * block, HEAD_SIZE), f32),
            pltpu.VMEM((2, HEAD_SIZE, 2 * TILE), f32),
            pltpu.VMEM((heads, 2, 2, block, HEAD_SIZE), bf16),
            back, back, back,
            pltpu.VMEM(output_rows.shape, bf16),
            pltpu.VMEM(output_rows.shape, bf16),
            pltpu.VMEM((parts, heads, 4, rows), f32),
            dma((heads, parts, 6)), dma((heads, parts, 6)), dma((heads, 6)),
            dma((parts,)), dma((parts,)), dma((2,)),
        ] + [dma((heads,))] * 10,
        compiler_params=pltpu.CompilerParams(
            collective_id=0, has_side_effects=True, vmem_limit_bytes=52 * 2 ** 20
        ),
        cost_estimate=pl.CostEstimate(
            flops=pair_ops * HEAD_SIZE * 10, bytes_accessed=16 * 2 ** 20, transcendentals=pair_ops
        ),
    )(rotated_queries, rotated_keys, value_matrix, output_gradient, output_rows, lse, docs)


def solution(mesh):
    return jax.shard_map(
        functools.partial(on_device, mesh.shape["seq"], mesh.shape["head"]),
        mesh=mesh,
        in_specs=(
            P(("seq", "head"), None),
            P(("seq", "head"), None),
            P(("seq", "head"), None),
            P(("seq", "head"), None),
            P(("seq", "head"), None),
            P(None, ("seq", "head")),
            P(),
        ),
        out_specs=(P("seq", "head"), P("seq", "head"), P("seq", "head")),
        check_vma=False,
    )
```

```python
import functools
import math

import jax
import jax.numpy as jnp
from jax import lax
from jax.experimental import pallas as pl
from jax.experimental.pallas import tpu as pltpu
from jax.sharding import PartitionSpec as P

HEAD_SIZE = 128
LOOKBACK_SPAN = 1024
TILE = 256
SCORE_SCALE = 168.0 ** (-0.5)
LOG2E = math.log2(math.e)
MASKED = -1e30
MESH = pl.DeviceIdType.MESH
KV_LEAD = 7
Q_LEAD = 2
HALO_LEAD = 5
KV_FIRST = 3


def dot(a, b, contract):
    return lax.dot_general(a, b, ((contract[:1], contract[1:]), ((), ())), preferred_element_type=jnp.float32)


def kernel(
    shards, parts, heads,
    q_hbm, k_hbm, v_hbm, do_hbm, o_hbm, lse_ref, docs_ref,
    dq_ref, dk_ref, dv_ref,
    kv, qd, stats, bias, own, acc, dqt, part, ret_a, ret_b, ret_c, o_buf, do_buf, st_src,
    y_send, y_recv, loc, st_send, st_recv, st_loc,
    near_send, near_recv, fardir_send, fwd_send, far_recv,
    p0_send, p1_send, a_recv, b_recv, c_recv,
):
    s = lax.axis_index("seq")
    y = lax.axis_index("head")
    even = lax.rem(s, 2) == 0
    rows = k_hbm.shape[0]
    block = rows * parts
    near_rows = pl.ds(block, block)
    far_rows = pl.ds(0, block)
    own_rows = pl.ds(2 * block, block)

    def at(seq, head):
        return {"seq": seq, "head": head}

    barrier = pltpu.get_barrier_semaphore()
    for step in range(1, parts):
        pl.semaphore_signal(barrier, inc=1, device_id=at(s, lax.rem(y + step, parts)), device_id_type=MESH)
    has_prev, has_next = s >= 1, s < shards - 1
    even_prev = even & (s >= 2)
    even_next = even & (s + 2 < shards)
    for cond, other in ((has_prev, s - 1), (has_next, s + 1), (even_prev, s - 2), (even_next, s + 2)):

        @pl.when(cond)
        def _():
            pl.semaphore_signal(barrier, inc=1, device_id=at(other, y), device_id_type=MESH)

    peers = parts - 1
    for cond in (has_prev, has_next, even_prev, even_next):
        peers = peers + jnp.where(cond, 1, 0)
    pl.semaphore_wait(barrier, peers)

    half = (y * rows) // TILE
    inner = pl.multiple_of(lax.rem(y * rows, TILE), rows)
    token_row = pl.multiple_of(2 * block + y * rows, rows)

    def pieces(g, target):
        head = target * heads + g
        col = pl.ds(pl.multiple_of(head * HEAD_SIZE, HEAD_SIZE), HEAD_SIZE)
        found = [
            (k_hbm.at[:, col], kv.at[g, 0, pl.ds(token_row, rows), :]),
            (v_hbm.at[:, col], kv.at[g, 1, pl.ds(token_row, rows), :]),
        ]
        for source, slot in ((q_hbm, 0), (do_hbm, 1)):
            for j in range(2):
                qcol = pl.ds(pl.multiple_of((head * 2 + j) * HEAD_SIZE, HEAD_SIZE), HEAD_SIZE)
                found.append((source.at[:, qcol], qd.at[g, slot, half, j, pl.ds(inner, rows), :]))
        return found

    def y_copies(g, which):
        found = []
        for step in range(1, parts):
            target = lax.rem(y + step, parts)
            for n, (src, dst) in enumerate(pieces(g, target)):
                if n in which:
                    found.append(
                        pltpu.make_async_remote_copy(
                            src_ref=src, dst_ref=dst,
                            send_sem=y_send.at[g, step, n], recv_sem=y_recv.at[g, step, n],
                            device_id=at(s, target), device_id_type=MESH,
                        )
                    )
        return found

    def local_copies(g, which):
        return [
            pltpu.make_async_copy(src, dst, loc.at[g, n])
            for n, (src, dst) in enumerate(pieces(g, y))
            if n in which
        ]

    KV_PIECES, Q_PIECES = (0, 1), (2, 3, 4, 5)

    def y_start(g, which):
        for copy in y_copies(g, which):
            copy.start()
        for copy in local_copies(g, which):
            copy.start()

    def y_arrive(g, which):
        for step in range(1, parts):
            source = lax.rem(y + parts - step, parts)
            their_half = (source * rows) // TILE
            their_inner = pl.multiple_of(lax.rem(source * rows, TILE), rows)
            their_row = pl.multiple_of(2 * block + source * rows, rows)
            for n, (src, _) in enumerate(pieces(g, y)):
                if n not in which:
                    continue
                if n < 2:
                    dst = kv.at[g, n, pl.ds(their_row, rows), :]
                else:
                    dst = qd.at[g, (n - 2) // 2, their_half, (n - 2) % 2, pl.ds(their_inner, rows), :]
                pltpu.make_async_remote_copy(
                    src_ref=src, dst_ref=dst,
                    send_sem=y_send.at[g, step, n], recv_sem=y_recv.at[g, step, n],
                    device_id=at(s, source), device_id_type=MESH,
                ).wait_recv()
        for copy in local_copies(g, which):
            copy.wait()

    def stat_copy(step, mine):
        other = lax.rem(y + step, parts)
        source = y if mine else lax.rem(y + parts - step, parts)
        return pltpu.make_async_remote_copy(
            src_ref=st_src.at[other], dst_ref=stats.at[source],
            send_sem=st_send.at[step], recv_sem=st_recv.at[step],
            device_id=at(s, other), device_id_type=MESH,
        )

    def remote(src, dst, send, recv, target):
        return pltpu.make_async_remote_copy(
            src_ref=src, dst_ref=dst, send_sem=send, recv_sem=recv,
            device_id=at(target, y), device_id_type=MESH,
        )

    def near(g):
        return remote(kv.at[g, :, own_rows, :], kv.at[g, :, near_rows, :], near_send.at[g], near_recv.at[g], s + 1)

    def far_direct(g):
        return remote(kv.at[g, :, own_rows, :], kv.at[g, :, far_rows, :], fardir_send.at[g], far_recv.at[g], s + 2)

    def far_forward(g):
        return remote(kv.at[g, :, near_rows, :], kv.at[g, :, far_rows, :], fwd_send.at[g], far_recv.at[g], s + 1)

    def back_far_even(g):
        return remote(part.at[g, 0], ret_b.at[g], p0_send.at[g], b_recv.at[g], s - 2)

    def back_far_odd(g):
        return remote(part.at[g, 0], ret_c.at[g], p0_send.at[g], c_recv.at[g], s - 1)

    def back_near(g):
        return remote(part.at[g, 1], ret_a.at[g], p1_send.at[g], a_recv.at[g], s - 1)

    def halo_send(g):
        y_arrive(g, KV_PIECES)

        @pl.when(has_next)
        def _():
            near(g).start()

        @pl.when(even_next)
        def _():
            far_direct(g).start()

    kv_lead, q_lead, halo_lead = (min(n, heads) for n in (KV_LEAD, Q_LEAD, HALO_LEAD))
    y_start(0, KV_PIECES)
    o_copy = pltpu.make_async_copy(o_hbm, o_buf, st_loc.at[0])
    do_copy = pltpu.make_async_copy(do_hbm, do_buf, st_loc.at[1])
    o_copy.start()
    do_copy.start()
    kv_first = min(KV_FIRST, heads)
    for g in range(1, kv_first):
        y_start(g, KV_PIECES)

    def fill_stats(p, target):
        @pl.loop(0, heads)
        def _(g):
            target[g, 0:2, :] = lse_ref[p, g] * LOG2E
            for j in range(2):
                cols = pl.ds(pl.multiple_of(((p * heads + g) * 2 + j) * HEAD_SIZE, HEAD_SIZE), HEAD_SIZE)
                product = o_buf[:, cols].astype(jnp.float32) * do_buf[:, cols].astype(jnp.float32)
                target[g, 2 + j:3 + j, :] = jnp.sum(product.T, axis=0, keepdims=True)

    halo_send(0)
    o_copy.wait()
    do_copy.wait()
    for step in range(1, parts):
        other = lax.rem(y + step, parts)
        fill_stats(other, st_src.at[other])
        stat_copy(step, True).start()
    started = 0
    for g in range(1, halo_lead):
        if kv_first + g - 1 < kv_lead:
            y_start(kv_first + g - 1, KV_PIECES)
        halo_send(g)
        if g % 2 == 1 and started < q_lead:
            y_start(started, Q_PIECES)
            started += 1
    for g in range(started, q_lead):
        y_start(g, Q_PIECES)
    for g in range(kv_first + halo_lead - 1, kv_lead):
        y_start(g, KV_PIECES)
    fill_stats(y, stats.at[y])

    for limit, row in ((2, 0), (1, block)):

        @pl.when(s < limit)
        def _():
            @pl.loop(0, heads)
            def _(g):
                kv[g, :, pl.ds(row, block), :] = jnp.zeros((2, block, HEAD_SIZE), kv.dtype)

    key_tiles = 3 * block // TILE
    reach = LOOKBACK_SPAN // TILE

    def pair_index(t, u):
        return u * (reach + 1) + (t - u)

    for t in range(key_tiles):
        key_doc = jnp.broadcast_to(docs_ref[:, t * TILE:(t + 1) * TILE].astype(jnp.float32), (TILE, TILE)).T
        for u in range(2):
            if not 0 <= t - u <= reach:
                continue
            first = 2 * block + u * TILE
            query_doc = docs_ref[:, first:first + TILE].astype(jnp.float32)
            gap = (
                (first - t * TILE)
                + lax.broadcasted_iota(jnp.int32, (TILE, TILE), 1)
                - lax.broadcasted_iota(jnp.int32, (TILE, TILE), 0)
            )
            allowed = (key_doc == query_doc) & (gap >= 0) & (gap < LOOKBACK_SPAN)
            bias[pair_index(t, u)] = jnp.where(allowed, 0.0, MASKED)

    for step in range(1, parts):
        stat_copy(step, False).wait_recv()

    sources = parts // 2

    def stat_row(g, u, kind):
        found = [
            stats[u * sources + i, g, kind * 2 + j:kind * 2 + j + 1, :]
            for j in range(2)
            for i in range(sources)
        ]
        return jnp.concatenate(found, axis=1) if len(found) > 1 else found[0]

    def tile(g, t, u):
        keys = kv[g, 0, t * TILE:(t + 1) * TILE, :]
        values = kv[g, 1, t * TILE:(t + 1) * TILE, :]
        queries = qd[g, 0, u].reshape(2 * TILE, HEAD_SIZE)
        grads = qd[g, 1, u].reshape(2 * TILE, HEAD_SIZE)
        mask = bias[pair_index(t, u)]
        scores = dot(keys, queries, (1, 1)) * (SCORE_SCALE * LOG2E) - stat_row(g, u, 0)
        prob = jnp.exp2(scores + jnp.concatenate([mask, mask], axis=1))
        prob_grad = dot(values, grads, (1, 1))
        score_grad = (SCORE_SCALE * prob * (prob_grad - stat_row(g, u, 1))).astype(jnp.bfloat16)
        dv = dot(prob.astype(jnp.bfloat16), grads, (1, 0))
        dk = dot(score_grad, queries, (1, 0))
        dq = dot(keys, score_grad, (0, 0))
        if t == u:
            dqt[u] = dq
        else:
            dqt[u] += dq
        first = u == 0 or t == reach + 1
        if t < 2 * block // TILE:
            target, row = acc, t * TILE
        else:
            target, row = own.at[g], t * TILE - 2 * block
        if first:
            target[0, row:row + TILE, :] = dk
            target[1, row:row + TILE, :] = dv
        else:
            target[0, row:row + TILE, :] += dk
            target[1, row:row + TILE, :] += dv

    def combine(g):
        back_far_odd(g).wait_recv()
        part[g, 1] = (part[g, 1].astype(jnp.float32) + ret_c[g].astype(jnp.float32)).astype(jnp.bfloat16)
        back_near(g).start()

    @pl.loop(0, heads)
    def _(g):
        @pl.when(g + kv_lead < heads)
        def _():
            y_start(g + kv_lead, KV_PIECES)

        @pl.when(g + q_lead < heads)
        def _():
            y_start(g + q_lead, Q_PIECES)

        @pl.when(g + halo_lead < heads)
        def _():
            halo_send(g + halo_lead)

        @pl.when(has_prev)
        def _():
            near(g).wait_recv()

        @pl.when(even_prev)
        def _():
            far_forward(g).start()

        y_arrive(g, Q_PIECES)

        @pl.when(s >= 2)
        def _():
            far_direct(g).wait_recv()

        own_tile = 2 * block // TILE
        for u in range(2):
            for t in range(u, own_tile):
                tile(g, t, u)
        part[g, 0] = acc[:, 0:block, :].astype(jnp.bfloat16)
        part[g, 1] = acc[:, block:2 * block, :].astype(jnp.bfloat16)

        @pl.when(even_prev)
        def _():
            back_far_even(g).start()

        @pl.when(jnp.logical_not(even))
        def _():
            back_near(g).start()

        @pl.when(jnp.logical_not(even) & (s >= 2))
        def _():
            back_far_odd(g).start()

        @pl.when(even_prev & (g >= 1))
        def _():
            combine(g - 1)

        for t, u in ((own_tile, 0), (own_tile, 1), (own_tile + 1, 1)):
            tile(g, t, u)
        for u in range(2):
            for j in range(2):
                head_cols = pl.ds(pl.multiple_of((g * 2 + j) * HEAD_SIZE, HEAD_SIZE), HEAD_SIZE)
                dq_ref[u * TILE:(u + 1) * TILE, head_cols] = (
                    dqt[u, :, j * TILE:(j + 1) * TILE].T.astype(jnp.bfloat16)
                )

    @pl.when(even_prev)
    def _():
        combine(heads - 1)

    @pl.loop(0, heads)
    def _(g):
        @pl.when(has_next)
        def _():
            back_near(g).wait_recv()
            own[g] += ret_a[g].astype(jnp.float32)

        @pl.when(even_next)
        def _():
            back_far_even(g).wait_recv()
            own[g] += ret_b[g].astype(jnp.float32)

        cols = pl.ds(pl.multiple_of(g * HEAD_SIZE, HEAD_SIZE), HEAD_SIZE)
        dk_ref[:, cols] = own[g, 0].astype(jnp.bfloat16)
        dv_ref[:, cols] = own[g, 1].astype(jnp.bfloat16)

    @pl.loop(0, heads)
    def _(g):
        for copy in y_copies(g, KV_PIECES + Q_PIECES):
            copy.wait_send()

        @pl.when(has_next)
        def _():
            near(g).wait_send()

        @pl.when(even_next)
        def _():
            far_direct(g).wait_send()

        @pl.when(even_prev)
        def _():
            far_forward(g).wait_send()

        @pl.when(s >= 2)
        def _():
            back_far_even(g).wait_send()

        @pl.when(has_prev)
        def _():
            back_near(g).wait_send()

    for step in range(1, parts):
        stat_copy(step, True).wait_send()


def on_device(
    shards, parts,
    rotated_queries, rotated_keys, value_matrix, output_rows, output_gradient, softmax_log_total, doc_ids,
):
    rows = rotated_queries.shape[0]
    key_heads = rotated_keys.shape[1] // HEAD_SIZE
    heads = key_heads // parts
    block = rows * parts
    lse = softmax_log_total.reshape(parts, heads, 2, rows)
    padded = jnp.concatenate([jnp.full((LOOKBACK_SPAN,), -1, doc_ids.dtype), doc_ids])
    docs = lax.dynamic_slice_in_dim(padded, lax.axis_index("seq") * block, 3 * block, 0)[None, :]

    any_spec = pl.BlockSpec(memory_space=pl.ANY)
    vmem = pl.BlockSpec(memory_space=pltpu.VMEM)
    dma = pltpu.SemaphoreType.DMA
    bf16, f32 = jnp.bfloat16, jnp.float32
    back = pltpu.VMEM((heads, 2, block, HEAD_SIZE), bf16)
    pairs = 2 * (LOOKBACK_SPAN // TILE + 1)
    pair_ops = heads * pairs * TILE * 2 * TILE
    return pl.pallas_call(
        functools.partial(kernel, shards, parts, heads),
        out_shape=(
            jax.ShapeDtypeStruct((block, heads * 2 * HEAD_SIZE), bf16),
            jax.ShapeDtypeStruct((block, heads * HEAD_SIZE), bf16),
            jax.ShapeDtypeStruct((block, heads * HEAD_SIZE), bf16),
        ),
        in_specs=[any_spec] * 5 + [vmem, vmem],
        out_specs=(vmem, vmem, vmem),
        scratch_shapes=[
            pltpu.VMEM((heads, 2, 3 * block, HEAD_SIZE), bf16),
            pltpu.VMEM((heads, 2, 2, 2, TILE, HEAD_SIZE), bf16),
            pltpu.VMEM((parts, heads, 4, rows), f32),
            pltpu.VMEM((pairs, TILE, TILE), f32),
            pltpu.VMEM((heads, 2, block, HEAD_SIZE), f32),
            pltpu.VMEM((2, 2 * block, HEAD_SIZE), f32),
            pltpu.VMEM((2, HEAD_SIZE, 2 * TILE), f32),
            pltpu.VMEM((heads, 2, 2, block, HEAD_SIZE), bf16),
            back, back, back,
            pltpu.VMEM(output_rows.shape, bf16),
            pltpu.VMEM(output_rows.shape, bf16),
            pltpu.VMEM((parts, heads, 4, rows), f32),
            dma((heads, parts, 6)), dma((heads, parts, 6)), dma((heads, 6)),
            dma((parts,)), dma((parts,)), dma((2,)),
        ] + [dma((heads,))] * 10,
        compiler_params=pltpu.CompilerParams(
            collective_id=0, has_side_effects=True, vmem_limit_bytes=52 * 2 ** 20
        ),
        cost_estimate=pl.CostEstimate(
            flops=pair_ops * HEAD_SIZE * 10, bytes_accessed=16 * 2 ** 20, transcendentals=pair_ops
        ),
    )(rotated_queries, rotated_keys, value_matrix, output_gradient, output_rows, lse, docs)


def solution(mesh):
    return jax.shard_map(
        functools.partial(on_device, mesh.shape["seq"], mesh.shape["head"]),
        mesh=mesh,
        in_specs=(
            P(("seq", "head"), None),
            P(("seq", "head"), None),
            P(("seq", "head"), None),
            P(("seq", "head"), None),
            P(("seq", "head"), None),
            P(None, ("seq", "head")),
            P(),
        ),
        out_specs=(P("seq", "head"), P("seq", "head"), P("seq", "head")),
        check_vma=False,
    )
```
